32 devices in a mesh: replica: 2 (over y), mp: 16 (over z, x, core).
Axes of the slice: x: 2, y: 2, z: 4, core: 2. Of those that a mesh axis runs over, the one named last changes fastest.
Arguments:
- owner_shard: int32 [64, 256], P(('replica', 'mp')), may hold values from 0 to 15, as said below
- slot_index: int32 [64, 256], P(('replica', 'mp')), may hold values from 0 to 127
- lengths: int32 [64], P(('replica', 'mp')), may hold values from 32 to 256
- labels: float32 [64, 256], P(('replica', 'mp')), may hold values from 0 to 1
- embed_table: bfloat16 [32768, 256], P('mp'), may hold values from -3 to 3
- accumulator: float32 [32768], P('mp'), may hold values from 0.1 to 10
- touched: int32 [2048], P('mp'), may hold values from 0 to 2047, as said below
- w_in: bfloat16 [256, 1024], replicated, may hold values from -0.375 to 0.375
- w_mid: bfloat16 [1024, 1024], replicated, may hold values from -0.1875 to 0.1875
- norm_gain: float32 [1024], replicated, may hold values from 0.5 to 2
- w_out: float32 [1024], replicated, may hold values from -0.1875 to 0.1875
Outputs:
- table_out: bfloat16 [32768, 256], P('mp')
- accum_out: float32 [32768], P('mp')
The draws below stay inside these ranges and needn't reach their ends.
Inputs may be any that keep to these rules, and one draw needn't show every extreme that they name: `owner_shard`: among the events of one device, every shard is named at most 64 times, and one shard, the same for all devices, is named exactly 64 times by every device. `touched`: the 128 entries of each shard are distinct rows of that shard.
All inputs are finite; a program needn't handle non-finite values.
Results may differ from the reference program's by a relative error of at most 0.0034.
Values may be sent and summed in bfloat16 or wider, within the bound.
No kernel may reach another device: no remote copies, remote signals or barrier semaphores. Data moves between devices by JAX's collectives and lax.ppermute only.
A program may use at most 64 MiB of HBM per device.

```python
import math
import jax
import jax.numpy as jnp
import numpy as np
from jax import lax

E = 256
H = 1024
ROWS_SHARD = 2048
TOUCH = 128
LEN = 256
SAMP_DEV = 2
CAP = 64
SAMPLES = 64
VOCAB = 32768
N_REPLICA = 2
N_MP = 16


def draw_owner_shard(key, part):
    block_count = N_REPLICA * N_MP
    events = SAMP_DEV * LEN
    grid_size = N_MP * CAP
    hot_shard = jax.random.randint(jax.random.fold_in(key, 7), (), 0, N_MP)
    block_keys = jax.random.split(jax.random.fold_in(key, 11), block_count)

    def one_block(block_key):
        key_score, key_order = jax.random.split(block_key)
        grid = jnp.arange(grid_size, dtype=jnp.int32)
        grid_owner = grid // CAP
        scores = jax.random.randint(key_score, (grid_size,), 0, 1 << 18) * grid_size + grid
        scores = jnp.where(grid_owner == hot_shard, -1 - grid, scores)
        order = jnp.argsort(scores)
        chosen = grid_owner[order[:events]]
        return jax.random.permutation(key_order, chosen)
    return jax.vmap(one_block)(block_keys).reshape(SAMPLES, LEN).astype(jnp.int32)


def draw_touched(key, part):
    shard_keys = jax.random.split(jax.random.fold_in(key, 3), N_MP)

    def one_shard(shard_key):
        return jax.random.permutation(shard_key, ROWS_SHARD)[:TOUCH]
    return jax.vmap(one_shard)(shard_keys).reshape(N_MP * TOUCH).astype(jnp.int32)


def with_ends(array, own_key, smallest, high):
    longest = array.shape.index(max(array.shape))
    spots = []
    for shift in (0, 1):
        where = [jax.random.randint(jax.random.fold_in(own_key, axis), (), 0, length) for axis, length in enumerate(array.shape)]
        where[longest] = (where[longest] + shift) % array.shape[longest]
        spots.append(tuple(where))
    return array.at[spots[0]].set(smallest).at[spots[1]].set(high)


def level_of(rng, shape, cuts, smallest, largest):
    factor_of, own = 1.0, jax.random.fold_in(rng, 6)
    for position, shards_of in cuts:
        draws = jnp.exp(jax.random.uniform(jax.random.fold_in(own, position), (shards_of,), jnp.float32, smallest / len(cuts), largest / len(cuts)))
        factor_of = factor_of * jnp.repeat(draws, shape[position] // shards_of).reshape([-1 if axis == position else 1 for axis in range(len(shape))])
    return factor_of


def cumulative_ranks(amount, slope):
    loads = [(1 << 20) // math.isqrt(standing ** slope) + 1 for standing in range(1, amount + 1)]
    spread = 1 + sum(loads) // (1 << 30)
    return np.cumsum(np.array([max(1, weight // spread) for weight in loads]))


def ranked(own_key, extent, number_of, skew):
    table = cumulative_ranks(number_of, skew)
    ticket = jax.random.randint(jax.random.fold_in(own_key, 1), extent, 0, int(table[number_of - 1]))
    standing = jnp.searchsorted(jnp.asarray(table, jnp.int32), ticket, side="right")
    return jax.random.permutation(jax.random.fold_in(own_key, 2), number_of)[standing].astype(jnp.int32)


def bell_draw(rng, dims, width, most, shards=(), held_as=jnp.bfloat16):
    factor_of = level_of(rng, dims, shards, -0.22, 0.18) if shards else 1.0
    drawn = jax.random.normal(rng, dims, jnp.float32) * width * factor_of
    return jnp.minimum(jnp.maximum(drawn, -most), most).astype(held_as)


def setup_inputs(seed: int = 0) -> dict:
    splits = jax.random.split(jax.random.key(seed), 12)
    return {
        "owner_shard": draw_owner_shard(jax.random.fold_in(splits[11], 71), 0),
        "slot_index": with_ends(ranked(splits[1], (SAMPLES, LEN), TOUCH, 2), jax.random.fold_in(splits[1], 3), 0, TOUCH - 1).astype(jnp.int32),
        "lengths": with_ends(jax.random.randint(splits[2], (SAMPLES,), LEN // 8, LEN + 1), jax.random.fold_in(splits[2], 1), LEN // 8, LEN).astype(jnp.int32),
        "labels": jnp.clip(1.0 * jax.random.uniform(splits[3], (SAMPLES, LEN), jnp.float32) ** level_of(splits[3], (SAMPLES, LEN), ((0, 32),), -0.2, 0.2), 0.0, 1.0),
        "embed_table": bell_draw(splits[4], (VOCAB, E), 0.5, 3.0, ((0, 16),)),
        "accumulator": jnp.clip(jnp.exp(math.log(10.0) - 4.6051702 * jax.random.uniform(splits[5], (VOCAB,), jnp.float32) ** level_of(splits[5], (VOCAB,), ((0, 16),), -0.2, 0.2)), 0.1, 10.0),
        "touched": draw_touched(jax.random.fold_in(splits[11], 71), 0),
        "w_in": bell_draw(splits[7], (E, H), E ** -0.5, 0.375),
        "w_mid": bell_draw(splits[8], (H, H), H ** -0.5, 0.1875),
        "norm_gain": jnp.clip(jnp.exp(jax.random.uniform(splits[9], (H,), jnp.float32, math.log(0.5), math.log(2.0))), 0.5, 2.0),
        "w_out": bell_draw(splits[10], (H,), H ** -0.5, 0.1875, (), jnp.float32),
    }


learn_rate = 1.0

def silu_slope(values):
    sigma_val = jax.nn.sigmoid(values)
    return sigma_val * (1.0 + values * (1.0 - sigma_val))

def encoder_grad(looked_up, labels, live_mask, w_in, w_mid, norm_gain, w_out):
    pre_act = jnp.dot(looked_up, w_in, preferred_element_type=jnp.float32)
    hidden = jax.nn.silu(pre_act)
    inv_rms = lax.rsqrt(lax.optimization_barrier(jnp.mean(hidden * hidden, axis=-1, keepdims=True)) + 1e-06)
    normed = (hidden * inv_rms * norm_gain).astype(jnp.bfloat16)
    mixed = jnp.dot(normed, w_mid, preferred_element_type=jnp.float32)
    output = hidden + jax.nn.silu(mixed)
    logits = lax.optimization_barrier(jnp.sum(output * w_out, axis=-1))
    d_logit = (jax.nn.sigmoid(logits) - labels) * live_mask
    d_output = d_logit[:, None] * w_out
    d_mixed = (d_output * silu_slope(mixed)).astype(jnp.bfloat16)
    d_normed = jnp.dot(d_mixed, w_mid.T, preferred_element_type=jnp.float32)
    gained = d_normed * norm_gain
    d_hidden = d_output + inv_rms * gained - hidden * inv_rms ** 3 * lax.optimization_barrier(jnp.mean(hidden * gained, axis=-1, keepdims=True))
    d_pre = (d_hidden * silu_slope(pre_act)).astype(jnp.bfloat16)
    return jnp.dot(d_pre, w_in.T, preferred_element_type=jnp.float32).astype(jnp.bfloat16)

def reference(owner_shard, slot_index, lengths, labels, embed_table, accumulator, touched, w_in, w_mid, norm_gain, w_out):
    owners = owner_shard.reshape(-1).astype(jnp.int32)
    slots = slot_index.reshape(-1).astype(jnp.int32)
    list_pos = owners * TOUCH + slots
    row_id = owners * ROWS_SHARD + touched[list_pos]
    looked_up = embed_table[row_id].reshape(SAMPLES, LEN, E)
    live_mask = (jnp.arange(LEN, dtype=jnp.int32)[None, :] < lengths[:, None]).astype(jnp.float32)

    def one_sample(pieces):
        return encoder_grad(pieces[0], pieces[1], pieces[2], w_in, w_mid, norm_gain, w_out)
    event_grad = lax.map(one_sample, (looked_up, labels, live_mask))
    grad_sum = jax.ops.segment_sum(event_grad.reshape(-1, E).astype(jnp.float32), list_pos, num_segments=N_MP * TOUCH)
    global_rows = (jnp.arange(N_MP, dtype=jnp.int32)[:, None] * ROWS_SHARD + touched.reshape(N_MP, TOUCH)).reshape(-1)
    acc_new = accumulator[global_rows] + lax.optimization_barrier(jnp.sum(grad_sum * grad_sum, axis=1))
    new_rows = embed_table[global_rows].astype(jnp.float32) - learn_rate * grad_sum * lax.rsqrt(acc_new)[:, None]
    table_out = embed_table.at[global_rows].set(new_rows.astype(jnp.bfloat16))
    accum_out = accumulator.at[global_rows].set(acc_new)
    return (table_out, accum_out)
```

```python
import jax
import jax.numpy as jnp
from jax import lax
from jax.experimental import pallas as pl
from jax.experimental.pallas import tpu as pltpu
from jax.sharding import PartitionSpec as P


learn_rate = 1.0
F32 = jnp.float32
BF16 = jnp.bfloat16
WHOLE = pl.BlockSpec(memory_space=pltpu.VMEM)
SCALARS = pl.BlockSpec(memory_space=pltpu.SMEM)


def split3(values):
    high = values.astype(BF16)
    rest = values - high.astype(F32)
    middle = rest.astype(BF16)
    low = (rest - middle.astype(F32)).astype(BF16)
    return high, middle, low


def dot_rows(left, right):
    return lax.dot_general(left, right, (((1,), (1,)), ((), ())), preferred_element_type=F32)


def eye(size):
    return lax.broadcasted_iota(jnp.int32, (size, size), 0) == lax.broadcasted_iota(
        jnp.int32, (size, size), 1
    )


def to_column(row):
    size = row.shape[1]
    return jnp.sum(jnp.where(eye(size), row, jnp.zeros_like(row)), axis=1, keepdims=True)


def to_row(column):
    size = column.shape[0]
    return jnp.sum(jnp.where(eye(size), column, jnp.zeros_like(column)), axis=0, keepdims=True)


def event_sums_kernel(lengths_ref, owner_ref, slot_ref, label_ref, out_ref):
    samples, length = owner_ref.shape
    shards = out_ref.shape[1]
    touch = out_ref.shape[2] // 2
    total = jnp.zeros((4 * shards, touch), F32)
    for s in range(samples):
        place = lax.broadcasted_iota(jnp.int32, (shards, length), 1)
        shard = lax.broadcasted_iota(jnp.int32, (shards, length), 0)
        chosen = (owner_ref[s : s + 1, :] == shard) & (place < lengths_ref[s])
        slot = lax.broadcasted_iota(jnp.int32, (touch, length), 0)
        slots = jnp.where(slot_ref[s : s + 1, :] == slot, 1.0, 0.0).astype(BF16)
        labels = jnp.where(chosen, label_ref[s : s + 1, :], 0.0)
        left = jnp.concatenate([jnp.where(chosen, 1.0, 0.0).astype(BF16), *split3(labels)], axis=0)
        total = total + dot_rows(left, slots)
    count = total[:shards]
    label_sum = total[shards : 2 * shards] + total[2 * shards : 3 * shards] + total[3 * shards :]
    for r in range(out_ref.shape[0]):
        out_ref[r, :, :touch] = count
        out_ref[r, :, touch:] = label_sum


def encoder_kernel(
    touched_ref,
    table_ref,
    acc_ref,
    w_in_ref,
    w_mid_ref,
    gain_ref,
    w_out_ref,
    base_ref,
    old_ref,
    grad_ref,
    stats_ref,
):
    rows, _ = table_ref.shape
    touched = touched_ref[...]
    touch = touched.shape[1]
    picks = jnp.where(
        lax.broadcasted_iota(jnp.int32, (touch, rows), 1) == to_column(touched), 1.0, 0.0
    ).astype(BF16)
    old = jnp.dot(picks, table_ref[...], preferred_element_type=F32).astype(BF16)
    old_ref[...] = old

    gain = gain_ref[...]
    w_out = w_out_ref[...]
    pre = jnp.dot(old, w_in_ref[...], preferred_element_type=F32)
    sig_pre = jax.nn.sigmoid(pre)
    hidden = pre * sig_pre
    inv_rms = lax.rsqrt(jnp.mean(hidden * hidden, axis=-1, keepdims=True) + 1e-06)
    normed = (hidden * inv_rms * gain).astype(BF16)
    mixed = jnp.dot(normed, w_mid_ref[...], preferred_element_type=F32)
    sig_mixed = jax.nn.sigmoid(mixed)
    output = hidden + mixed * sig_mixed
    logits = jnp.sum(output * w_out, axis=-1, keepdims=True)
    d_mixed = (w_out * (sig_mixed * (1.0 + mixed * (1.0 - sig_mixed)))).astype(BF16)
    gained = dot_rows(d_mixed, w_mid_ref[...]) * gain
    d_hidden = (
        w_out
        + inv_rms * gained
        - hidden * inv_rms**3 * jnp.mean(hidden * gained, axis=-1, keepdims=True)
    )
    d_pre = (d_hidden * (sig_pre * (1.0 + pre * (1.0 - sig_pre)))).astype(BF16)
    grad = dot_rows(d_pre, w_in_ref[...])
    grad_ref[...] = grad

    acc = acc_ref[...]
    blocks, lanes = acc.shape
    in_lane = (lax.broadcasted_iota(jnp.int32, (lanes, touch), 0) == touched % lanes)
    in_block = lax.broadcasted_iota(jnp.int32, (blocks, touch), 0) == touched // lanes
    lane_pick = jnp.where(in_lane, 1.0, 0.0).astype(BF16)
    found = sum(jnp.dot(part, lane_pick, preferred_element_type=F32) for part in split3(acc))
    stats_ref[0:1, :] = to_row(logits)
    stats_ref[1:2, :] = to_row(jnp.sum(grad * grad, axis=-1, keepdims=True))
    stats_ref[2:3, :] = jnp.sum(jnp.where(in_block, found, 0.0), axis=0, keepdims=True)

    step = min(rows, 256)
    for start in range(0, rows, step):
        spread = jnp.where(
            lax.broadcasted_iota(jnp.int32, (step, touch), 0) + start == touched, 1.0, 0.0
        )
        kept = jnp.sum(spread, axis=1, keepdims=True) == 0.0
        part = table_ref[start : start + step, :]
        base_ref[start : start + step, :] = jnp.where(kept, part.astype(F32), 0.0).astype(BF16)


def update_kernel(
    got_ref, stats_ref, touched_ref, acc_ref, old_ref, grad_ref, base_ref, table_ref, acc_out_ref,
    new_ref, sems,
):
    touched = touched_ref[...]
    touch = touched.shape[1]
    rows = base_ref.shape[0]
    summed = jnp.sum(got_ref[...], axis=0, keepdims=True)
    logits = stats_ref[0:1, :]
    d_logit = jax.nn.sigmoid(logits) * summed[:, :touch] - summed[:, touch:]
    acc_new = stats_ref[2:3, :] + d_logit * d_logit * stats_ref[1:2, :]
    factor = to_column(learn_rate * d_logit * lax.rsqrt(acc_new))
    new_rows = (old_ref[...].astype(F32) - factor * grad_ref[...]).astype(BF16)

    step = new_ref.shape[1]
    copies = []
    for part in range(rows // step):
        start = part * step
        spread = jnp.where(
            lax.broadcasted_iota(jnp.int32, (step, touch), 0) + start == touched, 1.0, 0.0
        ).astype(BF16)
        moved = jnp.dot(spread, new_rows, preferred_element_type=F32)
        new_ref[part] = (base_ref[start : start + step, :].astype(F32) + moved).astype(BF16)
        copy = pltpu.make_async_copy(
            new_ref.at[part], table_ref.at[pl.ds(start, step), :], sems.at[part]
        )
        copy.start()
        copies.append(copy)

    acc = acc_ref[...]
    blocks, lanes = acc.shape
    in_lane = lax.broadcasted_iota(jnp.int32, (lanes, touch), 0) == touched % lanes
    in_block = lax.broadcasted_iota(jnp.int32, (blocks, touch), 0) == touched // lanes
    lane_pick = jnp.where(in_lane, 1.0, 0.0).astype(BF16)
    block_pick = jnp.where(in_block, 1.0, 0.0).astype(BF16)
    left = jnp.concatenate(
        [block_pick, *split3(jnp.where(in_block, acc_new, 0.0))], axis=0
    )
    placed = dot_rows(left, lane_pick)
    written = placed[blocks : 2 * blocks] + placed[2 * blocks : 3 * blocks] + placed[3 * blocks :]
    acc_out_ref[...] = jnp.where(placed[:blocks] > 0.5, written, acc)
    for copy in copies:
        copy.wait()


def on_device(
    owner_shard,
    slot_index,
    lengths,
    labels,
    embed_table,
    accumulator,
    touched,
    w_in,
    w_mid,
    norm_gain,
    w_out,
):
    shards = lax.axis_size("mp")
    replicas = lax.axis_size("replica")
    rows, width = embed_table.shape
    touch = touched.shape[0]
    lanes = 128
    touched_row = touched.reshape(1, touch)
    acc = accumulator.reshape(rows // lanes, lanes)

    sums = pl.pallas_call(
        event_sums_kernel,
        out_shape=jax.ShapeDtypeStruct((replicas, shards, 2 * touch), F32),
        in_specs=[SCALARS, WHOLE, WHOLE, WHOLE],
        out_specs=WHOLE,
        name="event_sums",
    )(lengths, owner_shard, slot_index, labels)
    got = lax.all_to_all(
        sums.reshape(replicas * shards, 2 * touch), ("replica", "mp"), 0, 0, tiled=True
    )

    base, old, grad, stats = pl.pallas_call(
        encoder_kernel,
        out_shape=(
            jax.ShapeDtypeStruct((rows, width), BF16),
            jax.ShapeDtypeStruct((touch, width), BF16),
            jax.ShapeDtypeStruct((touch, width), F32),
            jax.ShapeDtypeStruct((8, touch), F32),
        ),
        in_specs=[WHOLE] * 7,
        out_specs=(WHOLE,) * 4,
        compiler_params=pltpu.CompilerParams(vmem_limit_bytes=24 * 1024 * 1024),
        cost_estimate=pl.CostEstimate(
            flops=1_000_000_000, bytes_accessed=5_000_000, transcendentals=300_000
        ),
        name="row_gradients",
    )(
        touched_row,
        embed_table,
        acc,
        w_in,
        w_mid,
        norm_gain.reshape(1, -1),
        w_out.reshape(1, -1),
    )

    step = min(rows, 512)
    table_out, acc_out = pl.pallas_call(
        update_kernel,
        out_shape=(
            jax.ShapeDtypeStruct((rows, width), BF16),
            jax.ShapeDtypeStruct(acc.shape, F32),
        ),
        in_specs=[WHOLE] * 7,
        out_specs=(pl.BlockSpec(memory_space=pl.ANY), WHOLE),
        scratch_shapes=[
            pltpu.VMEM((rows // step, step, width), BF16),
            pltpu.SemaphoreType.DMA((rows // step,)),
        ],
        compiler_params=pltpu.CompilerParams(vmem_limit_bytes=16 * 1024 * 1024),
        name="row_update",
    )(got, stats, touched_row, acc, old, grad, base)
    return (table_out, acc_out.reshape(rows))


def solution(mesh):
    in_specs = (
        P(("replica", "mp"), None),
        P(("replica", "mp"), None),
        P(("replica", "mp")),
        P(("replica", "mp"), None),
        P("mp", None),
        P("mp"),
        P("mp"),
        P(),
        P(),
        P(),
        P(),
    )
    out_specs = (P("mp", None), P("mp"))
    return jax.shard_map(
        on_device, mesh=mesh, in_specs=in_specs, out_specs=out_specs, check_vma=False
    )
```

```python
import functools

import jax
import jax.numpy as jnp
from jax import lax
from jax.experimental import pallas as pl
from jax.experimental.pallas import tpu as pltpu
from jax.sharding import PartitionSpec as P


learn_rate = 1.0
F32 = jnp.float32
BF16 = jnp.bfloat16
WHOLE = pl.BlockSpec(memory_space=pltpu.VMEM)
IN_HBM = pl.BlockSpec(memory_space=pltpu.HBM)


def split3(values):
    high = values.astype(BF16)
    rest = values - high.astype(F32)
    middle = rest.astype(BF16)
    low = (rest - middle.astype(F32)).astype(BF16)
    return high, middle, low


def dot_rows(left, right):
    return lax.dot_general(left, right, (((1,), (1,)), ((), ())), preferred_element_type=F32)


def eye(size):
    return lax.broadcasted_iota(jnp.int32, (size, size), 0) == lax.broadcasted_iota(
        jnp.int32, (size, size), 1
    )


def to_column(row):
    size = row.shape[1]
    return jnp.sum(jnp.where(eye(size), row, jnp.zeros_like(row)), axis=1, keepdims=True)


def to_row(column):
    size = column.shape[0]
    return jnp.sum(jnp.where(eye(size), column, jnp.zeros_like(column)), axis=0, keepdims=True)


def event_sums_kernel(shards, lengths_ref, owner_ref, slot_ref, label_ref, out_ref):
    samples, length = owner_ref.shape
    touch = out_ref.shape[2] // 2
    total = jnp.zeros((4 * shards, touch), F32)
    for s in range(samples):
        place = lax.broadcasted_iota(jnp.int32, (shards, length), 1)
        shard = lax.broadcasted_iota(jnp.int32, (shards, length), 0)
        chosen = (owner_ref[s : s + 1, :] == shard) & (place < lengths_ref[:, s : s + 1])
        slot = lax.broadcasted_iota(jnp.int32, (touch, length), 0)
        slots = jnp.where(slot_ref[s : s + 1, :] == slot, 1.0, 0.0).astype(BF16)
        labels = jnp.where(chosen, label_ref[s : s + 1, :], 0.0)
        left = jnp.concatenate([jnp.where(chosen, 1.0, 0.0).astype(BF16), *split3(labels)], axis=0)
        total = total + dot_rows(left, slots)
    count = total[:shards]
    label_sum = total[shards : 2 * shards] + total[2 * shards : 3 * shards] + total[3 * shards :]
    for r in range(out_ref.shape[0] // shards):
        out_ref[r * shards : (r + 1) * shards, 0, :touch] = count
        out_ref[r * shards : (r + 1) * shards, 0, touch:] = label_sum


def row_gradients_kernel(
    touched_hbm,
    table_hbm,
    acc_hbm,
    w_in_hbm,
    w_mid_hbm,
    gain_hbm,
    w_out_hbm,
    table_ref,
    spread_ref,
    old_ref,
    grad_ref,
    stats_ref,
    acc_ref,
    touched_ref,
    w_in_ref,
    w_mid_ref,
    gain_ref,
    w_out_ref,
    sems,
):
    copies = [
        pltpu.make_async_copy(source, target, sems.at[i])
        for i, (source, target) in enumerate(
            (
                (touched_hbm, touched_ref),
                (table_hbm, table_ref),
                (w_in_hbm, w_in_ref),
                (gain_hbm, gain_ref),
                (w_mid_hbm, w_mid_ref),
                (w_out_hbm, w_out_ref),
                (acc_hbm, acc_ref),
            )
        )
    ]
    for copy in copies:
        copy.start()
    touched_copy, table_copy, w_in_copy, gain_copy, w_mid_copy, w_out_copy, acc_copy = copies

    rows = table_ref.shape[0]
    touched_copy.wait()
    touched = touched_ref[...]
    touch = touched.shape[1]
    picks = jnp.where(
        lax.broadcasted_iota(jnp.int32, (touch, rows), 1) == to_column(touched), 1.0, 0.0
    ).astype(BF16)
    table_copy.wait()
    old = jnp.dot(picks, table_ref[...], preferred_element_type=F32).astype(BF16)
    old_ref[...] = old

    w_in_copy.wait()
    pre = jnp.dot(old, w_in_ref[...], preferred_element_type=F32)
    sig_pre = jax.nn.sigmoid(pre)
    hidden = pre * sig_pre
    inv_rms = lax.rsqrt(jnp.mean(hidden * hidden, axis=-1, keepdims=True) + 1e-06)
    gain_copy.wait()
    gain = gain_ref[...]
    normed = (hidden * inv_rms * gain).astype(BF16)
    w_mid_copy.wait()
    mixed = jnp.dot(normed, w_mid_ref[...], preferred_element_type=F32)
    sig_mixed = jax.nn.sigmoid(mixed)
    output = hidden + mixed * sig_mixed
    w_out_copy.wait()
    w_out = w_out_ref[...]
    logits = jnp.sum(output * w_out, axis=-1, keepdims=True)
    d_mixed = (w_out * (sig_mixed * (1.0 + mixed * (1.0 - sig_mixed)))).astype(BF16)
    gained = dot_rows(d_mixed, w_mid_ref[...]) * gain
    d_hidden = (
        w_out
        + inv_rms * gained
        - hidden * inv_rms**3 * jnp.mean(hidden * gained, axis=-1, keepdims=True)
    )
    d_pre = (d_hidden * (sig_pre * (1.0 + pre * (1.0 - sig_pre)))).astype(BF16)
    grad = dot_rows(d_pre, w_in_ref[...])
    grad_ref[...] = grad

    acc_copy.wait()
    acc = acc_ref[...]
    blocks, lanes = acc.shape
    in_lane = lax.broadcasted_iota(jnp.int32, (lanes, touch), 0) == touched % lanes
    in_block = lax.broadcasted_iota(jnp.int32, (blocks, touch), 0) == touched // lanes
    lane_pick = jnp.where(in_lane, 1.0, 0.0).astype(BF16)
    found = sum(jnp.dot(part, lane_pick, preferred_element_type=F32) for part in split3(acc))
    stats_ref[0:1, :] = to_row(logits)
    stats_ref[1:2, :] = to_row(jnp.sum(grad * grad, axis=-1, keepdims=True))
    stats_ref[2:3, :] = jnp.sum(jnp.where(in_block, found, 0.0), axis=0, keepdims=True)
    stats_ref[3:4, :] = touched.astype(F32)

    step = min(rows, 256)
    for start in range(0, rows, step):
        spread = jnp.where(
            lax.broadcasted_iota(jnp.int32, (step, touch), 0) + start == touched, 1.0, 0.0
        )
        spread_ref[start : start + step, :] = spread.astype(BF16)
        kept = jnp.sum(spread, axis=1, keepdims=True) == 0.0
        part = table_ref[start : start + step, :]
        table_ref[start : start + step, :] = jnp.where(kept, part.astype(F32), 0.0).astype(BF16)


def row_update_kernel(
    got_ref, stats_ref, acc_ref, old_ref, grad_ref, spread_ref, base_ref, table_hbm, acc_hbm,
    new_ref, new_acc_ref, sems,
):
    rows, touch = spread_ref.shape
    step = new_ref.shape[1]
    parts = rows // step
    summed = jnp.sum(got_ref[...], axis=0)
    logits = stats_ref[0:1, :]
    d_logit = jax.nn.sigmoid(logits) * summed[:, :touch] - summed[:, touch:]
    acc_new = stats_ref[2:3, :] + d_logit * d_logit * stats_ref[1:2, :]

    factor = to_column(learn_rate * d_logit * lax.rsqrt(acc_new))
    new_rows = (old_ref[...].astype(F32) - factor * grad_ref[...]).astype(BF16)
    copies = []
    for part in range(parts):
        start = part * step
        moved = jnp.dot(
            spread_ref[start : start + step, :], new_rows, preferred_element_type=F32
        )
        new_ref[part] = base_ref[start : start + step, :] + moved.astype(BF16)
        copy = pltpu.make_async_copy(
            new_ref.at[part], table_hbm.at[pl.ds(start, step), :], sems.at[part]
        )
        copy.start()
        copies.append(copy)

    touched = stats_ref[3:4, :].astype(jnp.int32)
    acc = acc_ref[...]
    blocks, lanes = acc.shape
    in_lane = lax.broadcasted_iota(jnp.int32, (lanes, touch), 0) == touched % lanes
    in_block = lax.broadcasted_iota(jnp.int32, (blocks, touch), 0) == touched // lanes
    lane_pick = jnp.where(in_lane, 1.0, 0.0).astype(BF16)
    block_pick = jnp.where(in_block, 1.0, 0.0).astype(BF16)
    left = jnp.concatenate([block_pick, *split3(jnp.where(in_block, acc_new, 0.0))], axis=0)
    placed = dot_rows(left, lane_pick)
    written = placed[blocks : 2 * blocks] + placed[2 * blocks : 3 * blocks] + placed[3 * blocks :]
    new_acc_ref[...] = jnp.where(placed[:blocks] > 0.5, written, acc)
    copy = pltpu.make_async_copy(new_acc_ref, acc_hbm, sems.at[parts])
    copy.start()
    copies.append(copy)
    for copy in copies:
        copy.wait()


def on_device(
    owner_shard,
    slot_index,
    lengths,
    labels,
    embed_table,
    accumulator,
    touched,
    w_in,
    w_mid,
    norm_gain,
    w_out,
):
    shards = lax.axis_size("mp")
    replicas = lax.axis_size("replica")
    rows, width = embed_table.shape
    touch = touched.shape[0]
    lanes = 128

    def stay(array):
        return pltpu.with_memory_space_constraint(array, pltpu.HBM)

    sums = pl.pallas_call(
        functools.partial(event_sums_kernel, shards),
        out_shape=pltpu.VMEM((replicas * shards, 1, 2 * touch), F32),
        in_specs=[WHOLE] * 4,
        out_specs=WHOLE,
        name="event_sums",
    )(stay(lengths.reshape(1, -1)), stay(owner_shard), stay(slot_index), stay(labels))
    got = lax.all_to_all(sums, ("replica", "mp"), 0, 0, tiled=True)

    acc = accumulator.reshape(rows // lanes, lanes)
    gain_row = norm_gain.reshape(1, -1)
    w_out_row = w_out.reshape(1, -1)
    touched_row = touched.reshape(1, touch)
    base, spread, old, grad, stats, acc_copy = pl.pallas_call(
        row_gradients_kernel,
        out_shape=(
            pltpu.VMEM((rows, width), BF16),
            pltpu.VMEM((rows, touch), BF16),
            pltpu.VMEM((touch, width), BF16),
            pltpu.VMEM((touch, width), F32),
            pltpu.VMEM((8, touch), F32),
            pltpu.VMEM(acc.shape, F32),
        ),
        in_specs=[IN_HBM] * 7,
        out_specs=(WHOLE,) * 6,
        scratch_shapes=[
            pltpu.VMEM(touched_row.shape, jnp.int32),
            pltpu.VMEM(w_in.shape, BF16),
            pltpu.VMEM(w_mid.shape, BF16),
            pltpu.VMEM(gain_row.shape, F32),
            pltpu.VMEM(w_out_row.shape, F32),
            pltpu.SemaphoreType.DMA((7,)),
        ],
        compiler_params=pltpu.CompilerParams(vmem_limit_bytes=24 * 1024 * 1024),
        cost_estimate=pl.CostEstimate(
            flops=1_000_000_000, bytes_accessed=5_000_000, transcendentals=300_000
        ),
        name="row_gradients",
    )(
        stay(touched_row),
        stay(embed_table),
        stay(acc),
        stay(w_in),
        stay(w_mid),
        stay(gain_row),
        stay(w_out_row),
    )

    step = min(rows, 512)
    table_out, acc_out = pl.pallas_call(
        row_update_kernel,
        out_shape=(
            pltpu.HBM((rows, width), BF16),
            pltpu.HBM(acc.shape, F32),
        ),
        in_specs=[WHOLE] * 7,
        out_specs=(IN_HBM, IN_HBM),
        scratch_shapes=[
            pltpu.VMEM((rows // step, step, width), BF16),
            pltpu.VMEM(acc.shape, F32),
            pltpu.SemaphoreType.DMA((rows // step + 1,)),
        ],
        compiler_params=pltpu.CompilerParams(vmem_limit_bytes=16 * 1024 * 1024),
        name="row_update",
    )(got, stats, acc_copy, old, grad, spread, base)
    return (table_out, acc_out.reshape(rows))


def solution(mesh):
    in_specs = (
        P(("replica", "mp"), None),
        P(("replica", "mp"), None),
        P(("replica", "mp")),
        P(("replica", "mp"), None),
        P("mp", None),
        P("mp"),
        P("mp"),
        P(),
        P(),
        P(),
        P(),
    )
    out_specs = (P("mp", None), P("mp"))
    return jax.shard_map(
        on_device, mesh=mesh, in_specs=in_specs, out_specs=out_specs, check_vma=False
    )
```

```python
import functools

import jax
import jax.numpy as jnp
from jax import lax
from jax.experimental import pallas as pl
from jax.experimental.pallas import tpu as pltpu
from jax.sharding import PartitionSpec as P


learn_rate = 1.0
F32 = jnp.float32
BF16 = jnp.bfloat16
WHOLE = pl.BlockSpec(memory_space=pltpu.VMEM)
IN_HBM = pl.BlockSpec(memory_space=pltpu.HBM)


def split3(values):
    high = values.astype(BF16)
    rest = values - high.astype(F32)
    middle = rest.astype(BF16)
    low = (rest - middle.astype(F32)).astype(BF16)
    return high, middle, low


def dot_rows(left, right):
    return lax.dot_general(left, right, (((1,), (1,)), ((), ())), preferred_element_type=F32)


def eye(size):
    return lax.broadcasted_iota(jnp.int32, (size, size), 0) == lax.broadcasted_iota(
        jnp.int32, (size, size), 1
    )


def to_column(row):
    size = row.shape[1]
    return jnp.sum(jnp.where(eye(size), row, jnp.zeros_like(row)), axis=1, keepdims=True)


def to_row(column):
    size = column.shape[0]
    return jnp.sum(jnp.where(eye(size), column, jnp.zeros_like(column)), axis=0, keepdims=True)


def copies_of(pairs, sems):
    return [
        pltpu.make_async_copy(source, target, sems.at[i]) for i, (source, target) in enumerate(pairs)
    ]


def start_all(copies):
    for copy in copies:
        copy.start()


def place_in_mesh():
    replica, place = lax.axis_index("replica"), lax.axis_index("mp")
    replicas, places = lax.axis_size("replica"), lax.axis_size("mp")
    steps = replica + place // 4 + (place // 2) % 2
    most = replicas - 1 + (places - 1) // 4 + 1
    near = 5 * steps < 2 * most
    middle = jnp.logical_and(jnp.logical_not(near), 2 * steps < most)
    return near, middle


def event_sums(lengths_ref, owner_ref, slot_ref, label_ref, out_ref, shards):
    samples, length = owner_ref.shape
    touch = out_ref.shape[2] // 2
    total = jnp.zeros((4 * shards, touch), F32)
    for s in range(samples):
        place = lax.broadcasted_iota(jnp.int32, (shards, length), 1)
        shard = lax.broadcasted_iota(jnp.int32, (shards, length), 0)
        chosen = (owner_ref[s : s + 1, :] == shard) & (place < lengths_ref[:, s : s + 1])
        slot = lax.broadcasted_iota(jnp.int32, (touch, length), 0)
        slots = jnp.where(slot_ref[s : s + 1, :] == slot, 1.0, 0.0).astype(BF16)
        labels = jnp.where(chosen, label_ref[s : s + 1, :], 0.0)
        left = jnp.concatenate([jnp.where(chosen, 1.0, 0.0).astype(BF16), *split3(labels)], axis=0)
        total = total + dot_rows(left, slots)
    count = total[:shards]
    label_sum = total[shards : 2 * shards] + total[2 * shards : 3 * shards] + total[3 * shards :]
    for r in range(out_ref.shape[0] // shards):
        out_ref[r * shards : (r + 1) * shards, 0, :touch] = count
        out_ref[r * shards : (r + 1) * shards, 0, touch:] = label_sum


def pick_matrix(copies, touched_ref, rows):
    copies.touched.wait()
    touched = touched_ref[...]
    place = lax.broadcasted_iota(jnp.int32, (touched.shape[1], rows), 1)
    return jnp.where(place == to_column(touched), 1.0, 0.0).astype(BF16)


def look_up(copies, picks, table_ref, old_ref):
    copies.table.wait()
    old = jnp.dot(picks, table_ref[...], preferred_element_type=F32).astype(BF16)
    old_ref[...] = old
    return old


def forward(copies, old, w_in_ref, gain_ref):
    copies.w_in.wait()
    pre = jnp.dot(old, w_in_ref[...], preferred_element_type=F32)
    sig_pre = jax.nn.sigmoid(pre)
    hidden = pre * sig_pre
    inv_rms = lax.rsqrt(jnp.mean(hidden * hidden, axis=-1, keepdims=True) + 1e-06)
    copies.gain.wait()
    return pre, sig_pre, hidden, inv_rms


def mix(copies, hidden, inv_rms, gain_ref, w_mid_ref, w_out_ref, stats_ref):
    gain = gain_ref[...]
    normed = (hidden * inv_rms * gain).astype(BF16)
    copies.w_out.wait()
    w_out = w_out_ref[...]
    copies.w_mid.wait()
    features = w_mid_ref.shape[1]
    width = min(features, 256)
    weighted = jnp.zeros((hidden.shape[0], width), F32)
    d_mixed = []
    for start in range(0, features, width):
        part = slice(start, start + width)
        mixed = jnp.dot(normed, w_mid_ref[:, part], preferred_element_type=F32)
        sig_mixed = jax.nn.sigmoid(mixed)
        weighted = weighted + (hidden[:, part] + mixed * sig_mixed) * w_out[:, part]
        d_mixed.append(
            (w_out[:, part] * (sig_mixed * (1.0 + mixed * (1.0 - sig_mixed)))).astype(BF16)
        )
    stats_ref[0:1, :] = jax.nn.sigmoid(to_row(jnp.sum(weighted, axis=-1, keepdims=True)))
    return dot_rows(jnp.concatenate(d_mixed, axis=1), w_mid_ref[...]) * gain


def backward(state, gained, w_in_ref, w_out_ref, grad_ref, stats_ref):
    pre, sig_pre, hidden, inv_rms = state
    d_hidden = (
        w_out_ref[...]
        + inv_rms * gained
        - hidden * inv_rms**3 * jnp.mean(hidden * gained, axis=-1, keepdims=True)
    )
    d_pre = (d_hidden * (sig_pre * (1.0 + pre * (1.0 - sig_pre)))).astype(BF16)
    grad = dot_rows(d_pre, w_in_ref[...])
    grad_ref[...] = grad
    stats_ref[1:2, :] = to_row(jnp.sum(grad * grad, axis=-1, keepdims=True))


def lay_out(copies, touched_ref, spread_ref, acc_ref, stats_ref):
    rows = spread_ref.shape[0]
    touched = touched_ref[...]
    touch = touched.shape[1]
    spread_ref[...] = jnp.where(
        lax.broadcasted_iota(jnp.int32, (rows, touch), 0) == touched, 1.0, 0.0
    ).astype(BF16)
    copies.acc.wait()
    acc = acc_ref[...]
    blocks, lanes = acc.shape
    in_lane = lax.broadcasted_iota(jnp.int32, (lanes, touch), 0) == touched % lanes
    in_block = lax.broadcasted_iota(jnp.int32, (blocks, touch), 0) == touched // lanes
    lane_pick = jnp.where(in_lane, 1.0, 0.0).astype(BF16)
    found = sum(jnp.dot(part, lane_pick, preferred_element_type=F32) for part in split3(acc))
    stats_ref[2:3, :] = jnp.sum(jnp.where(in_block, found, 0.0), axis=0, keepdims=True)
    stats_ref[3:4, :] = touched.astype(F32)


def clear_rows(table_ref, spread_ref, old, base_ref):
    rows = table_ref.shape[0]
    step = min(rows, 256)
    for start in range(0, rows, step):
        part = slice(start, start + step)
        taken = jnp.dot(spread_ref[part, :], old, preferred_element_type=F32).astype(BF16)
        base_ref[part, :] = table_ref[part, :] - taken


def row_gradients(copies, held, weights):
    base_ref, spread_ref, old_ref, grad_ref, stats_ref, acc_ref = held
    touched_ref, w_in_ref, w_mid_ref, gain_ref, w_out_ref = weights
    picks = pick_matrix(copies, touched_ref, base_ref.shape[0])
    lay_out(copies, touched_ref, spread_ref, acc_ref, stats_ref)
    old = look_up(copies, picks, base_ref, old_ref)
    state = forward(copies, old, w_in_ref, gain_ref)
    gained = mix(copies, state[2], state[3], gain_ref, w_mid_ref, w_out_ref, stats_ref)
    backward(state, gained, w_in_ref, w_out_ref, grad_ref, stats_ref)
    clear_rows(base_ref, spread_ref, old, base_ref)


def row_update(got_ref, held, table_hbm, acc_hbm, new_ref, new_acc_ref, sems):
    base_ref, spread_ref, old_ref, grad_ref, stats_ref, acc_ref = held
    rows, touch = spread_ref.shape
    step = new_ref.shape[1]
    parts = rows // step
    summed = jnp.sum(got_ref[...], axis=0)
    d_logit = stats_ref[0:1, :] * summed[:, :touch] - summed[:, touch:]
    acc_new = stats_ref[2:3, :] + d_logit * d_logit * stats_ref[1:2, :]

    factor = jnp.broadcast_to(learn_rate * d_logit * lax.rsqrt(acc_new), (touch, touch)).T
    factor = jnp.concatenate([factor] * (grad_ref.shape[1] // touch), axis=1)
    new_rows = (old_ref[...].astype(F32) - factor * grad_ref[...]).astype(BF16)
    copies = []
    for part in range(parts):
        start = part * step
        moved = jnp.dot(
            spread_ref[start : start + step, :], new_rows, preferred_element_type=F32
        )
        new_ref[part] = base_ref[start : start + step, :] + moved.astype(BF16)
        copy = pltpu.make_async_copy(
            new_ref.at[part], table_hbm.at[pl.ds(start, step), :], sems.at[part]
        )
        copy.start()
        copies.append(copy)

    touched = stats_ref[3:4, :].astype(jnp.int32)
    acc = acc_ref[...]
    blocks, lanes = acc.shape
    in_lane = lax.broadcasted_iota(jnp.int32, (lanes, touch), 0) == touched % lanes
    in_block = lax.broadcasted_iota(jnp.int32, (blocks, touch), 0) == touched // lanes
    lane_pick = jnp.where(in_lane, 1.0, 0.0).astype(BF16)
    block_pick = jnp.where(in_block, 1.0, 0.0).astype(BF16)
    left = jnp.concatenate([block_pick, *split3(jnp.where(in_block, acc_new, 0.0))], axis=0)
    placed = dot_rows(left, lane_pick)
    written = placed[blocks : 2 * blocks] + placed[2 * blocks : 3 * blocks] + placed[3 * blocks :]
    new_acc_ref[...] = jnp.where(placed[:blocks] > 0.5, written, acc)
    copy = pltpu.make_async_copy(new_acc_ref, acc_hbm, sems.at[parts])
    copy.start()
    copies.append(copy)
    for copy in copies:
        copy.wait()


class RowCopies:
    def __init__(self, operands, held, weights, sems):
        touched_hbm, table_hbm, acc_hbm, w_in_hbm, w_mid_hbm, gain_hbm, w_out_hbm = operands
        touched_ref, w_in_ref, w_mid_ref, gain_ref, w_out_ref = weights
        self.small = copies_of(
            [
                (touched_hbm, touched_ref),
                (acc_hbm, held[5]),
                (gain_hbm, gain_ref),
                (w_out_hbm, w_out_ref),
            ],
            sems,
        )
        self.touched, self.acc, self.gain, self.w_out = self.small
        self.table = pltpu.make_async_copy(table_hbm, held[0], sems.at[4])
        self.w_in = pltpu.make_async_copy(w_in_hbm, w_in_ref, sems.at[5])
        self.w_mid = pltpu.make_async_copy(w_mid_hbm, w_mid_ref, sems.at[6])


def before_kernel(shards, *refs):
    event_operands, row_operands = refs[:4], refs[4:11]
    out_ref, held, gained_ref = refs[11], refs[12:18], refs[18]
    event_refs, weights = refs[19:23], refs[23:28]
    event_sems, row_sems = refs[28:]
    near, middle = place_in_mesh()
    not_far = jnp.logical_or(near, middle)
    event_copies = copies_of(zip(event_operands, event_refs), event_sems)
    copies = RowCopies(row_operands, held, weights, row_sems)
    start_all(event_copies)

    @pl.when(not_far)
    def _():
        start_all([*copies.small, copies.table, copies.w_in])

    for copy in event_copies:
        copy.wait()

    @pl.when(not_far)
    def _():
        copies.w_mid.start()

    event_sums(*event_refs, out_ref, shards)

    @pl.when(near)
    def _():
        row_gradients(copies, held, weights)

    @pl.when(middle)
    def _():
        touched_ref, w_in_ref, w_mid_ref, gain_ref, w_out_ref = weights
        picks = pick_matrix(copies, touched_ref, held[0].shape[0])
        old = look_up(copies, picks, held[0], held[2])
        state = forward(copies, old, w_in_ref, gain_ref)
        gained_ref[...] = mix(
            copies, state[2], state[3], gain_ref, w_mid_ref, w_out_ref, held[4]
        )
        copies.acc.wait()


def after_kernel(*refs):
    got_ref, held, gained_ref, row_operands = refs[0], refs[1:7], refs[7], refs[8:15]
    table_hbm, acc_hbm = refs[15:17]
    own_held, weights = refs[17:23], refs[23:28]
    new_ref, new_acc_ref, row_sems, out_sems = refs[28:]
    near, middle = place_in_mesh()
    not_near = jnp.logical_not(near)
    copies = RowCopies(row_operands, own_held, weights, row_sems)

    @pl.when(near)
    def _():
        row_update(got_ref, held, table_hbm, acc_hbm, new_ref, new_acc_ref, out_sems)

    @pl.when(middle)
    def _():
        start_all([*copies.small, copies.w_in])
        table_ref, _, old_ref, _, chances_ref, _ = held
        base_ref, spread_ref, own_old_ref, grad_ref, stats_ref, acc_ref = own_held
        touched_ref, w_in_ref, _, gain_ref, w_out_ref = weights
        old = old_ref[...]
        own_old_ref[...] = old
        stats_ref[0:1, :] = chances_ref[0:1, :]
        copies.touched.wait()
        lay_out(copies, touched_ref, spread_ref, acc_ref, stats_ref)
        clear_rows(table_ref, spread_ref, old, base_ref)
        state = forward(copies, old, w_in_ref, gain_ref)
        copies.w_out.wait()
        backward(state, gained_ref[...], w_in_ref, w_out_ref, grad_ref, stats_ref)

    @pl.when(jnp.logical_and(not_near, jnp.logical_not(middle)))
    def _():
        start_all([*copies.small, copies.table, copies.w_in, copies.w_mid])
        row_gradients(copies, own_held, weights)

    @pl.when(not_near)
    def _():
        row_update(got_ref, own_held, table_hbm, acc_hbm, new_ref, new_acc_ref, out_sems)


def on_device(
    owner_shard,
    slot_index,
    lengths,
    labels,
    embed_table,
    accumulator,
    touched,
    w_in,
    w_mid,
    norm_gain,
    w_out,
):
    shards = lax.axis_size("mp")
    replicas = lax.axis_size("replica")
    rows, width = embed_table.shape
    touch = touched.shape[0]
    lanes = 128

    def stay(array):
        return pltpu.with_memory_space_constraint(array, pltpu.HBM)

    def scratch(array):
        return pltpu.VMEM(array.shape, array.dtype)

    acc = accumulator.reshape(rows // lanes, lanes)
    gain_row = norm_gain.reshape(1, -1)
    w_out_row = w_out.reshape(1, -1)
    touched_row = touched.reshape(1, touch)
    event_operands = (lengths.reshape(1, -1), owner_shard, slot_index, labels)
    row_operands = (touched_row, embed_table, acc, w_in, w_mid, gain_row, w_out_row)
    held_shapes = [
        pltpu.VMEM((rows, width), BF16),
        pltpu.VMEM((rows, touch), BF16),
        pltpu.VMEM((touch, width), BF16),
        pltpu.VMEM((touch, width), F32),
        pltpu.VMEM((8, touch), F32),
        pltpu.VMEM(acc.shape, F32),
    ]
    weight_shapes = [scratch(array) for array in (touched_row, w_in, w_mid, gain_row, w_out_row)]
    memory = pltpu.CompilerParams(vmem_limit_bytes=32 * 1024 * 1024)

    gained_shape = pltpu.VMEM((touch, w_mid.shape[0]), F32)
    sums, *held = pl.pallas_call(
        functools.partial(before_kernel, shards),
        out_shape=(pltpu.VMEM((replicas * shards, 1, 2 * touch), F32), *held_shapes, gained_shape),
        in_specs=[IN_HBM] * 11,
        out_specs=(WHOLE,) * 8,
        scratch_shapes=[
            *[scratch(array) for array in event_operands],
            *weight_shapes,
            pltpu.SemaphoreType.DMA((4,)),
            pltpu.SemaphoreType.DMA((7,)),
        ],
        compiler_params=memory,
        name="before",
    )(*map(stay, event_operands), *map(stay, row_operands))
    got = lax.all_to_all(sums, ("replica", "mp"), 0, 0, tiled=True)

    step = min(rows, 512)
    table_out, acc_out = pl.pallas_call(
        after_kernel,
        out_shape=(pltpu.HBM((rows, width), BF16), pltpu.HBM(acc.shape, F32)),
        in_specs=[WHOLE] * 8 + [IN_HBM] * 7,
        out_specs=(IN_HBM, IN_HBM),
        scratch_shapes=[
            *held_shapes,
            *weight_shapes,
            pltpu.VMEM((rows // step, step, width), BF16),
            pltpu.VMEM(acc.shape, F32),
            pltpu.SemaphoreType.DMA((7,)),
            pltpu.SemaphoreType.DMA((rows // step + 1,)),
        ],
        compiler_params=memory,
        name="after",
    )(got, *held, *map(stay, row_operands))
    return (table_out, acc_out.reshape(rows))


def solution(mesh):
    in_specs = (
        P(("replica", "mp"), None),
        P(("replica", "mp"), None),
        P(("replica", "mp")),
        P(("replica", "mp"), None),
        P("mp", None),
        P("mp"),
        P("mp"),
        P(),
        P(),
        P(),
        P(),
    )
    out_specs = (P("mp", None), P("mp"))
    return jax.shard_map(
        on_device, mesh=mesh, in_specs=in_specs, out_specs=out_specs, check_vma=False
    )
```

```python
import functools

import jax
import jax.numpy as jnp
from jax import lax
from jax.experimental import pallas as pl
from jax.experimental.pallas import tpu as pltpu
from jax.sharding import PartitionSpec as P


learn_rate = 1.0
F32 = jnp.float32
BF16 = jnp.bfloat16
WHOLE = pl.BlockSpec(memory_space=pltpu.VMEM)
IN_HBM = pl.BlockSpec(memory_space=pltpu.HBM)


def split3(values):
    high = values.astype(BF16)
    rest = values - high.astype(F32)
    middle = rest.astype(BF16)
    low = (rest - middle.astype(F32)).astype(BF16)
    return high, middle, low


def dot_rows(left, right):
    return lax.dot_general(left, right, (((1,), (1,)), ((), ())), preferred_element_type=F32)


def eye(size):
    return lax.broadcasted_iota(jnp.int32, (size, size), 0) == lax.broadcasted_iota(
        jnp.int32, (size, size), 1
    )


def to_column(row):
    size = row.shape[1]
    return jnp.sum(jnp.where(eye(size), row, jnp.zeros_like(row)), axis=1, keepdims=True)


def to_row(column):
    size = column.shape[0]
    return jnp.sum(jnp.where(eye(size), column, jnp.zeros_like(column)), axis=0, keepdims=True)


def copies_of(pairs, sems):
    return [
        pltpu.make_async_copy(source, target, sems.at[i]) for i, (source, target) in enumerate(pairs)
    ]


def start_all(copies):
    for copy in copies:
        copy.start()


def place_in_mesh():
    replica, place = lax.axis_index("replica"), lax.axis_index("mp")
    replicas, places = lax.axis_size("replica"), lax.axis_size("mp")
    steps = replica + place // 4 + (place // 2) % 2
    most = replicas - 1 + (places - 1) // 4 + 1
    near = 5 * steps < 2 * most
    middle = jnp.logical_and(jnp.logical_not(near), 2 * steps < most)
    outer = jnp.logical_and(2 * steps >= most, 3 * steps < 2 * most)
    return near, middle, outer


def event_sums(lengths_ref, owner_ref, slot_ref, label_ref, out_ref, shards):
    samples, length = owner_ref.shape
    touch = out_ref.shape[2] // 2
    total = jnp.zeros((4 * shards, touch), F32)
    for s in range(samples):
        place = lax.broadcasted_iota(jnp.int32, (shards, length), 1)
        shard = lax.broadcasted_iota(jnp.int32, (shards, length), 0)
        chosen = (owner_ref[s : s + 1, :] == shard) & (place < lengths_ref[:, s : s + 1])
        slot = lax.broadcasted_iota(jnp.int32, (touch, length), 0)
        slots = jnp.where(slot_ref[s : s + 1, :] == slot, 1.0, 0.0).astype(BF16)
        labels = jnp.where(chosen, label_ref[s : s + 1, :], 0.0)
        left = jnp.concatenate([jnp.where(chosen, 1.0, 0.0).astype(BF16), *split3(labels)], axis=0)
        total = total + dot_rows(left, slots)
    count = total[:shards]
    label_sum = total[shards : 2 * shards] + total[2 * shards : 3 * shards] + total[3 * shards :]
    for r in range(out_ref.shape[0] // shards):
        out_ref[r * shards : (r + 1) * shards, 0, :touch] = count
        out_ref[r * shards : (r + 1) * shards, 0, touch:] = label_sum


def pick_matrix(copies, touched_ref, rows):
    copies.touched.wait()
    touched = touched_ref[...]
    place = lax.broadcasted_iota(jnp.int32, (touched.shape[1], rows), 1)
    return jnp.where(place == to_column(touched), 1.0, 0.0).astype(BF16)


def look_up(copies, picks, table_ref, old_ref):
    copies.table.wait()
    old = jnp.dot(picks, table_ref[...], preferred_element_type=F32).astype(BF16)
    old_ref[...] = old
    return old


def forward(copies, old, w_in_ref, gain_ref):
    copies.w_in.wait()
    pre = jnp.dot(old, w_in_ref[...], preferred_element_type=F32)
    sig_pre = jax.nn.sigmoid(pre)
    hidden = pre * sig_pre
    inv_rms = lax.rsqrt(jnp.mean(hidden * hidden, axis=-1, keepdims=True) + 1e-06)
    copies.gain.wait()
    return pre, sig_pre, hidden, inv_rms


def mix(copies, hidden, inv_rms, gain_ref, w_mid_ref, w_out_ref, stats_ref):
    gain = gain_ref[...]
    normed = (hidden * inv_rms * gain).astype(BF16)
    copies.w_out.wait()
    w_out = w_out_ref[...]
    copies.w_mid.wait()
    features = w_mid_ref.shape[1]
    width = min(features, 256)
    weighted = jnp.zeros((hidden.shape[0], width), F32)
    d_mixed = []
    for start in range(0, features, width):
        part = slice(start, start + width)
        mixed = jnp.dot(normed, w_mid_ref[:, part], preferred_element_type=F32)
        sig_mixed = jax.nn.sigmoid(mixed)
        weighted = weighted + (hidden[:, part] + mixed * sig_mixed) * w_out[:, part]
        d_mixed.append(
            (w_out[:, part] * (sig_mixed * (1.0 + mixed * (1.0 - sig_mixed)))).astype(BF16)
        )
    stats_ref[0:1, :] = jax.nn.sigmoid(to_row(jnp.sum(weighted, axis=-1, keepdims=True)))
    return dot_rows(jnp.concatenate(d_mixed, axis=1), w_mid_ref[...]) * gain


def backward(state, gained, w_in_ref, w_out_ref, grad_ref, stats_ref):
    pre, sig_pre, hidden, inv_rms = state
    d_hidden = (
        w_out_ref[...]
        + inv_rms * gained
        - hidden * inv_rms**3 * jnp.mean(hidden * gained, axis=-1, keepdims=True)
    )
    d_pre = (d_hidden * (sig_pre * (1.0 + pre * (1.0 - sig_pre)))).astype(BF16)
    grad = dot_rows(d_pre, w_in_ref[...])
    grad_ref[...] = grad
    stats_ref[1:2, :] = to_row(jnp.sum(grad * grad, axis=-1, keepdims=True))


def lay_out(copies, touched_ref, spread_ref, acc_ref, stats_ref):
    rows = spread_ref.shape[0]
    touched = touched_ref[...]
    touch = touched.shape[1]
    spread_ref[...] = jnp.where(
        lax.broadcasted_iota(jnp.int32, (rows, touch), 0) == touched, 1.0, 0.0
    ).astype(BF16)
    copies.acc.wait()
    acc = acc_ref[...]
    blocks, lanes = acc.shape
    in_lane = lax.broadcasted_iota(jnp.int32, (lanes, touch), 0) == touched % lanes
    in_block = lax.broadcasted_iota(jnp.int32, (blocks, touch), 0) == touched // lanes
    lane_pick = jnp.where(in_lane, 1.0, 0.0).astype(BF16)
    found = sum(jnp.dot(part, lane_pick, preferred_element_type=F32) for part in split3(acc))
    stats_ref[2:3, :] = jnp.sum(jnp.where(in_block, found, 0.0), axis=0, keepdims=True)
    stats_ref[3:4, :] = touched.astype(F32)


def clear_rows(table_ref, spread_ref, old, base_ref):
    rows = table_ref.shape[0]
    step = min(rows, 256)
    for start in range(0, rows, step):
        part = slice(start, start + step)
        taken = jnp.dot(spread_ref[part, :], old, preferred_element_type=F32).astype(BF16)
        base_ref[part, :] = table_ref[part, :] - taken


def row_gradients(copies, held, weights):
    base_ref, spread_ref, old_ref, grad_ref, stats_ref, acc_ref = held
    touched_ref, w_in_ref, w_mid_ref, gain_ref, w_out_ref = weights
    picks = pick_matrix(copies, touched_ref, base_ref.shape[0])
    lay_out(copies, touched_ref, spread_ref, acc_ref, stats_ref)
    old = look_up(copies, picks, base_ref, old_ref)
    state = forward(copies, old, w_in_ref, gain_ref)
    gained = mix(copies, state[2], state[3], gain_ref, w_mid_ref, w_out_ref, stats_ref)
    backward(state, gained, w_in_ref, w_out_ref, grad_ref, stats_ref)
    clear_rows(base_ref, spread_ref, old, base_ref)


def row_update(got_ref, held, table_hbm, acc_hbm, new_ref, new_acc_ref, sems):
    base_ref, spread_ref, old_ref, grad_ref, stats_ref, acc_ref = held
    rows, touch = spread_ref.shape
    step = new_ref.shape[1]
    parts = rows // step
    summed = jnp.sum(got_ref[...], axis=0)
    d_logit = stats_ref[0:1, :] * summed[:, :touch] - summed[:, touch:]
    acc_new = stats_ref[2:3, :] + d_logit * d_logit * stats_ref[1:2, :]

    factor = jnp.broadcast_to(learn_rate * d_logit * lax.rsqrt(acc_new), (touch, touch)).T
    factor = jnp.concatenate([factor] * (grad_ref.shape[1] // touch), axis=1)
    new_rows = (old_ref[...].astype(F32) - factor * grad_ref[...]).astype(BF16)
    copies = []
    for part in range(parts):
        start = part * step
        moved = jnp.dot(
            spread_ref[start : start + step, :], new_rows, preferred_element_type=F32
        )
        new_ref[part] = base_ref[start : start + step, :] + moved.astype(BF16)
        copy = pltpu.make_async_copy(
            new_ref.at[part], table_hbm.at[pl.ds(start, step), :], sems.at[part]
        )
        copy.start()
        copies.append(copy)

    touched = stats_ref[3:4, :].astype(jnp.int32)
    acc = acc_ref[...]
    blocks, lanes = acc.shape
    in_lane = lax.broadcasted_iota(jnp.int32, (lanes, touch), 0) == touched % lanes
    in_block = lax.broadcasted_iota(jnp.int32, (blocks, touch), 0) == touched // lanes
    lane_pick = jnp.where(in_lane, 1.0, 0.0).astype(BF16)
    block_pick = jnp.where(in_block, 1.0, 0.0).astype(BF16)
    left = jnp.concatenate([block_pick, *split3(jnp.where(in_block, acc_new, 0.0))], axis=0)
    placed = dot_rows(left, lane_pick)
    written = placed[blocks : 2 * blocks] + placed[2 * blocks : 3 * blocks] + placed[3 * blocks :]
    new_acc_ref[...] = jnp.where(placed[:blocks] > 0.5, written, acc)
    copy = pltpu.make_async_copy(new_acc_ref, acc_hbm, sems.at[parts])
    copy.start()
    copies.append(copy)
    for copy in copies:
        copy.wait()


class RowCopies:
    def __init__(self, operands, held, weights, sems):
        touched_hbm, table_hbm, acc_hbm, w_in_hbm, w_mid_hbm, gain_hbm, w_out_hbm = operands
        touched_ref, w_in_ref, w_mid_ref, gain_ref, w_out_ref = weights
        self.small = copies_of(
            [
                (touched_hbm, touched_ref),
                (acc_hbm, held[5]),
                (gain_hbm, gain_ref),
                (w_out_hbm, w_out_ref),
            ],
            sems,
        )
        self.touched, self.acc, self.gain, self.w_out = self.small
        self.table = pltpu.make_async_copy(table_hbm, held[0], sems.at[4])
        self.w_in = pltpu.make_async_copy(w_in_hbm, w_in_ref, sems.at[5])
        self.w_mid = pltpu.make_async_copy(w_mid_hbm, w_mid_ref, sems.at[6])


def before_kernel(shards, *refs):
    event_operands, row_operands = refs[:4], refs[4:11]
    out_ref, held, gained_ref = refs[11], refs[12:18], refs[18]
    event_refs, weights = refs[19:23], refs[23:28]
    event_sems, row_sems = refs[28:]
    near, middle, outer = place_in_mesh()
    not_far = jnp.logical_or(near, middle)
    event_copies = copies_of(zip(event_operands, event_refs), event_sems)
    copies = RowCopies(row_operands, held, weights, row_sems)
    start_all(event_copies)

    @pl.when(not_far)
    def _():
        start_all([*copies.small, copies.table, copies.w_in])

    @pl.when(outer)
    def _():
        start_all([copies.touched, copies.table])

    for copy in event_copies:
        copy.wait()

    @pl.when(not_far)
    def _():
        copies.w_mid.start()

    event_sums(*event_refs, out_ref, shards)

    @pl.when(near)
    def _():
        row_gradients(copies, held, weights)

    @pl.when(middle)
    def _():
        touched_ref, w_in_ref, w_mid_ref, gain_ref, w_out_ref = weights
        picks = pick_matrix(copies, touched_ref, held[0].shape[0])
        old = look_up(copies, picks, held[0], held[2])
        state = forward(copies, old, w_in_ref, gain_ref)
        gained_ref[...] = mix(
            copies, state[2], state[3], gain_ref, w_mid_ref, w_out_ref, held[4]
        )
        copies.acc.wait()

    @pl.when(outer)
    def _():
        picks = pick_matrix(copies, weights[0], held[0].shape[0])
        look_up(copies, picks, held[0], held[2])


def after_kernel(*refs):
    got_ref, held, gained_ref, row_operands = refs[0], refs[1:7], refs[7], refs[8:15]
    table_hbm, acc_hbm = refs[15:17]
    own_held, weights = refs[17:23], refs[23:28]
    new_ref, new_acc_ref, row_sems, out_sems = refs[28:]
    near, middle, outer = place_in_mesh()
    not_near = jnp.logical_not(near)
    inner = jnp.logical_or(near, middle)
    copies = RowCopies(row_operands, own_held, weights, row_sems)

    @pl.when(near)
    def _():
        row_update(got_ref, held, table_hbm, acc_hbm, new_ref, new_acc_ref, out_sems)

    @pl.when(middle)
    def _():
        start_all([*copies.small, copies.w_in])
        table_ref, _, old_ref, _, chances_ref, _ = held
        base_ref, spread_ref, own_old_ref, grad_ref, stats_ref, acc_ref = own_held
        touched_ref, w_in_ref, _, gain_ref, w_out_ref = weights
        old = old_ref[...]
        own_old_ref[...] = old
        stats_ref[0:1, :] = chances_ref[0:1, :]
        copies.touched.wait()
        lay_out(copies, touched_ref, spread_ref, acc_ref, stats_ref)
        clear_rows(table_ref, spread_ref, old, base_ref)
        state = forward(copies, old, w_in_ref, gain_ref)
        copies.w_out.wait()
        backward(state, gained_ref[...], w_in_ref, w_out_ref, grad_ref, stats_ref)

    @pl.when(outer)
    def _():
        start_all([*copies.small, copies.w_in, copies.w_mid])
        table_ref, _, old_ref, _, _, _ = held
        base_ref, spread_ref, own_old_ref, grad_ref, stats_ref, acc_ref = own_held
        touched_ref, w_in_ref, w_mid_ref, gain_ref, w_out_ref = weights
        old = old_ref[...]
        own_old_ref[...] = old
        copies.touched.wait()
        lay_out(copies, touched_ref, spread_ref, acc_ref, stats_ref)
        clear_rows(table_ref, spread_ref, old, base_ref)
        state = forward(copies, old, w_in_ref, gain_ref)
        gained = mix(copies, state[2], state[3], gain_ref, w_mid_ref, w_out_ref, stats_ref)
        backward(state, gained, w_in_ref, w_out_ref, grad_ref, stats_ref)

    @pl.when(jnp.logical_not(jnp.logical_or(inner, outer)))
    def _():
        start_all([*copies.small, copies.table, copies.w_in, copies.w_mid])
        row_gradients(copies, own_held, weights)

    @pl.when(not_near)
    def _():
        row_update(got_ref, own_held, table_hbm, acc_hbm, new_ref, new_acc_ref, out_sems)


def on_device(
    owner_shard,
    slot_index,
    lengths,
    labels,
    embed_table,
    accumulator,
    touched,
    w_in,
    w_mid,
    norm_gain,
    w_out,
):
    shards = lax.axis_size("mp")
    replicas = lax.axis_size("replica")
    rows, width = embed_table.shape
    touch = touched.shape[0]
    lanes = 128

    def stay(array):
        return pltpu.with_memory_space_constraint(array, pltpu.HBM)

    def scratch(array):
        return pltpu.VMEM(array.shape, array.dtype)

    acc = accumulator.reshape(rows // lanes, lanes)
    gain_row = norm_gain.reshape(1, -1)
    w_out_row = w_out.reshape(1, -1)
    touched_row = touched.reshape(1, touch)
    event_operands = (lengths.reshape(1, -1), owner_shard, slot_index, labels)
    row_operands = (touched_row, embed_table, acc, w_in, w_mid, gain_row, w_out_row)
    held_shapes = [
        pltpu.VMEM((rows, width), BF16),
        pltpu.VMEM((rows, touch), BF16),
        pltpu.VMEM((touch, width), BF16),
        pltpu.VMEM((touch, width), F32),
        pltpu.VMEM((8, touch), F32),
        pltpu.VMEM(acc.shape, F32),
    ]
    weight_shapes = [scratch(array) for array in (touched_row, w_in, w_mid, gain_row, w_out_row)]
    memory = pltpu.CompilerParams(vmem_limit_bytes=32 * 1024 * 1024)

    gained_shape = pltpu.VMEM((touch, w_mid.shape[0]), F32)
    sums, *held = pl.pallas_call(
        functools.partial(before_kernel, shards),
        out_shape=(pltpu.VMEM((replicas * shards, 1, 2 * touch), F32), *held_shapes, gained_shape),
        in_specs=[IN_HBM] * 11,
        out_specs=(WHOLE,) * 8,
        scratch_shapes=[
            *[scratch(array) for array in event_operands],
            *weight_shapes,
            pltpu.SemaphoreType.DMA((4,)),
            pltpu.SemaphoreType.DMA((7,)),
        ],
        compiler_params=memory,
        name="before",
    )(*map(stay, event_operands), *map(stay, row_operands))
    got = lax.all_to_all(sums, ("replica", "mp"), 0, 0, tiled=True)

    step = min(rows, 256)
    table_out, acc_out = pl.pallas_call(
        after_kernel,
        out_shape=(pltpu.HBM((rows, width), BF16), pltpu.HBM(acc.shape, F32)),
        in_specs=[WHOLE] * 8 + [IN_HBM] * 7,
        out_specs=(IN_HBM, IN_HBM),
        scratch_shapes=[
            *held_shapes,
            *weight_shapes,
            pltpu.VMEM((rows // step, step, width), BF16),
            pltpu.VMEM(acc.shape, F32),
            pltpu.SemaphoreType.DMA((7,)),
            pltpu.SemaphoreType.DMA((rows // step + 1,)),
        ],
        compiler_params=memory,
        name="after",
    )(got, *held, *map(stay, row_operands))
    return (table_out, acc_out.reshape(rows))


def solution(mesh):
    in_specs = (
        P(("replica", "mp"), None),
        P(("replica", "mp"), None),
        P(("replica", "mp")),
        P(("replica", "mp"), None),
        P("mp", None),
        P("mp"),
        P("mp"),
        P(),
        P(),
        P(),
        P(),
    )
    out_specs = (P("mp", None), P("mp"))
    return jax.shard_map(
        on_device, mesh=mesh, in_specs=in_specs, out_specs=out_specs, check_vma=False
    )
```

```python
import functools

import jax
import jax.numpy as jnp
from jax import lax
from jax.experimental import pallas as pl
from jax.experimental.pallas import tpu as pltpu
from jax.sharding import PartitionSpec as P


learn_rate = 1.0
F32 = jnp.float32
BF16 = jnp.bfloat16
WHOLE = pl.BlockSpec(memory_space=pltpu.VMEM)
IN_HBM = pl.BlockSpec(memory_space=pltpu.HBM)


def split3(values):
    high = values.astype(BF16)
    rest = values - high.astype(F32)
    middle = rest.astype(BF16)
    low = (rest - middle.astype(F32)).astype(BF16)
    return high, middle, low


def dot_rows(left, right):
    return lax.dot_general(left, right, (((1,), (1,)), ((), ())), preferred_element_type=F32)


def eye(size):
    return lax.broadcasted_iota(jnp.int32, (size, size), 0) == lax.broadcasted_iota(
        jnp.int32, (size, size), 1
    )


def to_column(row):
    size = row.shape[1]
    return jnp.sum(jnp.where(eye(size), row, jnp.zeros_like(row)), axis=1, keepdims=True)


def to_row(column):
    size = column.shape[0]
    return jnp.sum(jnp.where(eye(size), column, jnp.zeros_like(column)), axis=0, keepdims=True)


def copies_of(pairs, sems):
    return [
        pltpu.make_async_copy(source, target, sems.at[i]) for i, (source, target) in enumerate(pairs)
    ]


def start_all(copies):
    for copy in copies:
        copy.start()


def place_in_mesh():
    replica, place = lax.axis_index("replica"), lax.axis_index("mp")
    replicas, places = lax.axis_size("replica"), lax.axis_size("mp")
    steps = replica + place // 4 + (place // 2) % 2
    most = replicas - 1 + (places - 1) // 4 + 1
    near = 5 * steps < 2 * most
    middle = jnp.logical_and(jnp.logical_not(near), 2 * steps < most)
    return near, middle


def event_sums(lengths_ref, owner_ref, slot_ref, label_ref, out_ref, shards):
    samples, length = owner_ref.shape
    touch = out_ref.shape[2] // 2
    place = lax.broadcasted_iota(jnp.int32, (shards, length), 1)
    shard = lax.broadcasted_iota(jnp.int32, (shards, length), 0)
    slot = lax.broadcasted_iota(jnp.int32, (touch, length), 0)
    lefts, rights = [], []
    for s in range(samples):
        chosen = (owner_ref[s : s + 1, :] == shard) & (place < lengths_ref[:, s : s + 1])
        picked = jnp.where(chosen, 1.0, 0.0).astype(BF16)
        parts = [part * picked for part in split3(label_ref[s : s + 1, :])]
        lefts.append(jnp.concatenate([picked, *parts], axis=0))
        rights.append(jnp.where(slot_ref[s : s + 1, :] == slot, 1.0, 0.0).astype(BF16))
    total = dot_rows(jnp.concatenate(lefts, axis=1), jnp.concatenate(rights, axis=1))
    count = total[:shards]
    label_sum = total[shards : 2 * shards] + total[2 * shards : 3 * shards] + total[3 * shards :]
    for r in range(out_ref.shape[0] // shards):
        out_ref[r * shards : (r + 1) * shards, 0, :touch] = count
        out_ref[r * shards : (r + 1) * shards, 0, touch:] = label_sum


def pick_matrix(copies, touched_ref, rows):
    copies.touched.wait()
    touched = touched_ref[...]
    place = lax.broadcasted_iota(jnp.int32, (touched.shape[1], rows), 1)
    return jnp.where(place == to_column(touched), 1.0, 0.0).astype(BF16)


def look_up(copies, picks, table_ref, old_ref):
    copies.table.wait()
    old = jnp.dot(picks, table_ref[...], preferred_element_type=F32).astype(BF16)
    old_ref[...] = old
    return old


def forward(copies, old, w_in_ref, gain_ref):
    copies.w_in.wait()
    pre = jnp.dot(old, w_in_ref[...], preferred_element_type=F32)
    sig_pre = jax.nn.sigmoid(pre)
    hidden = pre * sig_pre
    inv_rms = lax.rsqrt(jnp.mean(hidden * hidden, axis=-1, keepdims=True) + 1e-06)
    copies.gain.wait()
    return pre, sig_pre, hidden, inv_rms


def mix(copies, hidden, inv_rms, gain_ref, w_mid_ref, w_out_ref, stats_ref):
    gain = gain_ref[...]
    normed = (hidden * inv_rms * gain).astype(BF16)
    copies.w_out.wait()
    w_out = w_out_ref[...]
    copies.w_mid.wait()
    features = w_mid_ref.shape[1]
    width = min(features, 256)
    weighted = jnp.zeros((hidden.shape[0], width), F32)
    d_mixed = []
    for start in range(0, features, width):
        part = slice(start, start + width)
        mixed = jnp.dot(normed, w_mid_ref[:, part], preferred_element_type=F32)
        sig_mixed = jax.nn.sigmoid(mixed)
        weighted = weighted + (hidden[:, part] + mixed * sig_mixed) * w_out[:, part]
        d_mixed.append(
            (w_out[:, part] * (sig_mixed * (1.0 + mixed * (1.0 - sig_mixed)))).astype(BF16)
        )
    stats_ref[0:1, :] = jax.nn.sigmoid(to_row(jnp.sum(weighted, axis=-1, keepdims=True)))
    return dot_rows(jnp.concatenate(d_mixed, axis=1), w_mid_ref[...]) * gain


def backward(state, gained, w_in_ref, w_out_ref, grad_ref, stats_ref):
    pre, sig_pre, hidden, inv_rms = state
    d_hidden = (
        w_out_ref[...]
        + inv_rms * gained
        - hidden * inv_rms**3 * jnp.mean(hidden * gained, axis=-1, keepdims=True)
    )
    d_pre = (d_hidden * (sig_pre * (1.0 + pre * (1.0 - sig_pre)))).astype(BF16)
    grad = dot_rows(d_pre, w_in_ref[...])
    grad_ref[...] = grad
    stats_ref[1:2, :] = to_row(jnp.sum(grad * grad, axis=-1, keepdims=True))


def lay_out(copies, touched_ref, spread_ref, acc_ref, stats_ref):
    rows = spread_ref.shape[0]
    touched = touched_ref[...]
    touch = touched.shape[1]
    spread_ref[...] = jnp.where(
        lax.broadcasted_iota(jnp.int32, (rows, touch), 0) == touched, 1.0, 0.0
    ).astype(BF16)
    copies.acc.wait()
    acc = acc_ref[...]
    blocks, lanes = acc.shape
    in_lane = lax.broadcasted_iota(jnp.int32, (lanes, touch), 0) == touched % lanes
    in_block = lax.broadcasted_iota(jnp.int32, (blocks, touch), 0) == touched // lanes
    lane_pick = jnp.where(in_lane, 1.0, 0.0).astype(BF16)
    found = sum(jnp.dot(part, lane_pick, preferred_element_type=F32) for part in split3(acc))
    stats_ref[2:3, :] = jnp.sum(jnp.where(in_block, found, 0.0), axis=0, keepdims=True)
    stats_ref[3:4, :] = touched.astype(F32)


def clear_rows(table_ref, spread_ref, old, base_ref):
    rows = table_ref.shape[0]
    step = min(rows, 256)
    for start in range(0, rows, step):
        part = slice(start, start + step)
        taken = jnp.dot(spread_ref[part, :], old, preferred_element_type=F32).astype(BF16)
        base_ref[part, :] = table_ref[part, :] - taken


def row_gradients(copies, held, weights):
    base_ref, spread_ref, old_ref, grad_ref, stats_ref, acc_ref = held
    touched_ref, w_in_ref, w_mid_ref, gain_ref, w_out_ref = weights
    picks = pick_matrix(copies, touched_ref, base_ref.shape[0])
    lay_out(copies, touched_ref, spread_ref, acc_ref, stats_ref)
    old = look_up(copies, picks, base_ref, old_ref)
    state = forward(copies, old, w_in_ref, gain_ref)
    gained = mix(copies, state[2], state[3], gain_ref, w_mid_ref, w_out_ref, stats_ref)
    backward(state, gained, w_in_ref, w_out_ref, grad_ref, stats_ref)
    clear_rows(base_ref, spread_ref, old, base_ref)


def row_update(got_ref, held, table_hbm, acc_hbm, new_ref, new_acc_ref, sems):
    base_ref, spread_ref, old_ref, grad_ref, stats_ref, acc_ref = held
    rows, touch = spread_ref.shape
    step = new_ref.shape[1]
    parts = rows // step
    summed = jnp.sum(got_ref[...], axis=0)
    d_logit = stats_ref[0:1, :] * summed[:, :touch] - summed[:, touch:]
    acc_new = stats_ref[2:3, :] + d_logit * d_logit * stats_ref[1:2, :]

    factor = jnp.broadcast_to(learn_rate * d_logit * lax.rsqrt(acc_new), (touch, touch)).T
    factor = jnp.concatenate([factor] * (grad_ref.shape[1] // touch), axis=1)
    new_rows = (old_ref[...].astype(F32) - factor * grad_ref[...]).astype(BF16)
    copies = []
    for part in range(parts):
        start = part * step
        moved = jnp.dot(
            spread_ref[start : start + step, :], new_rows, preferred_element_type=F32
        )
        new_ref[part] = base_ref[start : start + step, :] + moved.astype(BF16)
        copy = pltpu.make_async_copy(
            new_ref.at[part], table_hbm.at[pl.ds(start, step), :], sems.at[part]
        )
        copy.start()
        copies.append(copy)

    touched = stats_ref[3:4, :].astype(jnp.int32)
    acc = acc_ref[...]
    blocks, lanes = acc.shape
    in_lane = lax.broadcasted_iota(jnp.int32, (lanes, touch), 0) == touched % lanes
    in_block = lax.broadcasted_iota(jnp.int32, (blocks, touch), 0) == touched // lanes
    lane_pick = jnp.where(in_lane, 1.0, 0.0).astype(BF16)
    block_pick = jnp.where(in_block, 1.0, 0.0).astype(BF16)
    left = jnp.concatenate([block_pick, *split3(jnp.where(in_block, acc_new, 0.0))], axis=0)
    placed = dot_rows(left, lane_pick)
    written = placed[blocks : 2 * blocks] + placed[2 * blocks : 3 * blocks] + placed[3 * blocks :]
    new_acc_ref[...] = jnp.where(placed[:blocks] > 0.5, written, acc)
    copy = pltpu.make_async_copy(new_acc_ref, acc_hbm, sems.at[parts])
    copy.start()
    copies.append(copy)
    for copy in copies:
        copy.wait()


class RowCopies:
    def __init__(self, operands, held, weights, sems):
        touched_hbm, table_hbm, acc_hbm, w_in_hbm, w_mid_hbm, gain_hbm, w_out_hbm = operands
        touched_ref, w_in_ref, w_mid_ref, gain_ref, w_out_ref = weights
        self.small = copies_of(
            [
                (touched_hbm, touched_ref),
                (acc_hbm, held[5]),
                (gain_hbm, gain_ref),
                (w_out_hbm, w_out_ref),
            ],
            sems,
        )
        self.touched, self.acc, self.gain, self.w_out = self.small
        self.table = pltpu.make_async_copy(table_hbm, held[0], sems.at[4])
        self.w_in = pltpu.make_async_copy(w_in_hbm, w_in_ref, sems.at[5])
        self.w_mid = pltpu.make_async_copy(w_mid_hbm, w_mid_ref, sems.at[6])


def before_kernel(shards, *refs):
    event_operands, row_operands = refs[:4], refs[4:11]
    out_ref, held, gained_ref = refs[11], refs[12:18], refs[18]
    event_refs, weights = refs[19:23], refs[23:28]
    event_sems, row_sems = refs[28:]
    near, middle = place_in_mesh()
    not_far = jnp.logical_or(near, middle)
    event_copies = copies_of(zip(event_operands, event_refs), event_sems)
    copies = RowCopies(row_operands, held, weights, row_sems)
    start_all(event_copies)

    @pl.when(not_far)
    def _():
        start_all([*copies.small, copies.table, copies.w_in])

    for copy in event_copies:
        copy.wait()

    @pl.when(not_far)
    def _():
        copies.w_mid.start()

    event_sums(*event_refs, out_ref, shards)

    @pl.when(near)
    def _():
        row_gradients(copies, held, weights)

    @pl.when(middle)
    def _():
        touched_ref, w_in_ref, w_mid_ref, gain_ref, w_out_ref = weights
        picks = pick_matrix(copies, touched_ref, held[0].shape[0])
        old = look_up(copies, picks, held[0], held[2])
        state = forward(copies, old, w_in_ref, gain_ref)
        gained_ref[...] = mix(
            copies, state[2], state[3], gain_ref, w_mid_ref, w_out_ref, held[4]
        )
        copies.acc.wait()


def after_kernel(*refs):
    got_ref, held, gained_ref, row_operands = refs[0], refs[1:7], refs[7], refs[8:15]
    table_hbm, acc_hbm = refs[15:17]
    own_held, weights = refs[17:23], refs[23:28]
    new_ref, new_acc_ref, row_sems, out_sems = refs[28:]
    near, middle = place_in_mesh()
    not_near = jnp.logical_not(near)
    copies = RowCopies(row_operands, own_held, weights, row_sems)

    @pl.when(near)
    def _():
        row_update(got_ref, held, table_hbm, acc_hbm, new_ref, new_acc_ref, out_sems)

    @pl.when(middle)
    def _():
        start_all([*copies.small, copies.w_in])
        table_ref, _, old_ref, _, chances_ref, _ = held
        base_ref, spread_ref, own_old_ref, grad_ref, stats_ref, acc_ref = own_held
        touched_ref, w_in_ref, _, gain_ref, w_out_ref = weights
        old = old_ref[...]
        own_old_ref[...] = old
        stats_ref[0:1, :] = chances_ref[0:1, :]
        copies.touched.wait()
        lay_out(copies, touched_ref, spread_ref, acc_ref, stats_ref)
        clear_rows(table_ref, spread_ref, old, base_ref)
        state = forward(copies, old, w_in_ref, gain_ref)
        copies.w_out.wait()
        backward(state, gained_ref[...], w_in_ref, w_out_ref, grad_ref, stats_ref)

    @pl.when(jnp.logical_and(not_near, jnp.logical_not(middle)))
    def _():
        start_all([*copies.small, copies.table, copies.w_in, copies.w_mid])
        row_gradients(copies, own_held, weights)

    @pl.when(not_near)
    def _():
        row_update(got_ref, own_held, table_hbm, acc_hbm, new_ref, new_acc_ref, out_sems)


def on_device(
    owner_shard,
    slot_index,
    lengths,
    labels,
    embed_table,
    accumulator,
    touched,
    w_in,
    w_mid,
    norm_gain,
    w_out,
):
    shards = lax.axis_size("mp")
    replicas = lax.axis_size("replica")
    rows, width = embed_table.shape
    touch = touched.shape[0]
    lanes = 128

    def stay(array):
        return pltpu.with_memory_space_constraint(array, pltpu.HBM)

    def scratch(array):
        return pltpu.VMEM(array.shape, array.dtype)

    acc = accumulator.reshape(rows // lanes, lanes)
    gain_row = norm_gain.reshape(1, -1)
    w_out_row = w_out.reshape(1, -1)
    touched_row = touched.reshape(1, touch)
    event_operands = (lengths.reshape(1, -1), owner_shard, slot_index, labels)
    row_operands = (touched_row, embed_table, acc, w_in, w_mid, gain_row, w_out_row)
    held_shapes = [
        pltpu.VMEM((rows, width), BF16),
        pltpu.VMEM((rows, touch), BF16),
        pltpu.VMEM((touch, width), BF16),
        pltpu.VMEM((touch, width), F32),
        pltpu.VMEM((8, touch), F32),
        pltpu.VMEM(acc.shape, F32),
    ]
    weight_shapes = [scratch(array) for array in (touched_row, w_in, w_mid, gain_row, w_out_row)]
    memory = pltpu.CompilerParams(vmem_limit_bytes=32 * 1024 * 1024)

    gained_shape = pltpu.VMEM((touch, w_mid.shape[0]), F32)
    sums, *held = pl.pallas_call(
        functools.partial(before_kernel, shards),
        out_shape=(pltpu.VMEM((replicas * shards, 1, 2 * touch), F32), *held_shapes, gained_shape),
        in_specs=[IN_HBM] * 11,
        out_specs=(WHOLE,) * 8,
        scratch_shapes=[
            *[scratch(array) for array in event_operands],
            *weight_shapes,
            pltpu.SemaphoreType.DMA((4,)),
            pltpu.SemaphoreType.DMA((7,)),
        ],
        compiler_params=memory,
        name="before",
    )(*map(stay, event_operands), *map(stay, row_operands))
    got = lax.all_to_all(sums, ("replica", "mp"), 0, 0, tiled=True)

    step = min(rows, 256)
    table_out, acc_out = pl.pallas_call(
        after_kernel,
        out_shape=(pltpu.HBM((rows, width), BF16), pltpu.HBM(acc.shape, F32)),
        in_specs=[WHOLE] * 8 + [IN_HBM] * 7,
        out_specs=(IN_HBM, IN_HBM),
        scratch_shapes=[
            *held_shapes,
            *weight_shapes,
            pltpu.VMEM((rows // step, step, width), BF16),
            pltpu.VMEM(acc.shape, F32),
            pltpu.SemaphoreType.DMA((7,)),
            pltpu.SemaphoreType.DMA((rows // step + 1,)),
        ],
        compiler_params=memory,
        name="after",
    )(got, *held, *map(stay, row_operands))
    return (table_out, acc_out.reshape(rows))


def solution(mesh):
    in_specs = (
        P(("replica", "mp"), None),
        P(("replica", "mp"), None),
        P(("replica", "mp")),
        P(("replica", "mp"), None),
        P("mp", None),
        P("mp"),
        P("mp"),
        P(),
        P(),
        P(),
        P(),
    )
    out_specs = (P("mp", None), P("mp"))
    return jax.shard_map(
        on_device, mesh=mesh, in_specs=in_specs, out_specs=out_specs, check_vma=False
    )
```
